32 devices in a mesh: dev: 32 (over z, y, x, core).
Axes of the slice: x: 2, y: 2, z: 4, core: 2. Of those that a mesh axis runs over, the one named last changes fastest.
Arguments:
- states: float32 [188, 262144], P(None, 'dev'), may hold values from -6 to 6
- particle_mass: float32 [262144], P('dev'), may hold values from 1 to 10
- bin_index: int32 [262144], P('dev'), may hold values from 0 to 3
- cell_index: int32 [262144], P('dev'), may hold values from 0 to 255, as said below
- move_slot: int32 [262144], P('dev'), may hold values from -1 to 1023, as said below
- react_list: int32 [65536], P('dev'), may hold values from -1 to 8191, as said below
- rate_weights: bfloat16 [939, 188], replicated, may hold values from -0.4375 to 0.4375
- stoichiometry: bfloat16 [188, 939], replicated, may hold values from -0.1875 to 0.1875
- rate_scale: float32 [939], replicated, may hold values from 0.2 to 2
- jacobian_inverse: bfloat16 [4, 188, 188], replicated, may hold values from -1 to 2
- mixing_rate: float32 [8192], P('dev'), may hold values from 0.5 to 8
Outputs:
- mixed_states: float32 [188, 294912], P(None, 'dev')
- cell_means: float32 [188, 8192], P(None, 'dev')
The draws below stay inside these ranges and needn't reach their ends.
Inputs may be any that keep to these rules, and one draw needn't show every extreme that they name: `move_slot`: on each device the entries that are not -1 are distinct. Entries below 512 never stand on device 0 and entries of 512 or more never on the last device. At most 512 particles of one device go each way, and that many go down from some device and up from some device. Every cell of every device keeps at least one staying particle. `cell_index`: for a staying particle, its cell on its own device; for a moving one, its cell on the device it moves to. `react_list`: each device lists distinct particles of its own first, then -1. A quarter of the devices list 2048 particles, the others 2048 // 4.
All inputs are finite; a program needn't handle non-finite values.
Results may differ from the reference program's by a relative error of at most 0.00089.
Values sent between devices are 32-bit elements; how exact they have to be, the bound alone decides.
A program may use at most 128 MiB of HBM per device.

```python
import math
import jax
import jax.numpy as jnp
from jax import lax

S = 188
R = 939
NB = 4
NEWTON = 3
P_DEV = 8192
MCAP = 512
C_DEV = 256
R_MAX = 2048
HELP_DEV = 896
NLOC = 9216
PARTICLES = 262144
CELLS = 8192
N_DEV = 32


def chemistry_lists(key):
    base = jax.random.fold_in(key, 7)
    heavy = jax.random.permutation(jax.random.fold_in(base, 1), N_DEV) < N_DEV // 4
    counts = jnp.where(heavy, R_MAX, R_MAX // 4).astype(jnp.int32)
    device_ids = jnp.arange(N_DEV, dtype=jnp.int32)

    def shuffled(device):
        return jax.random.permutation(jax.random.fold_in(jax.random.fold_in(base, 2), device), P_DEV)[:R_MAX]
    chosen = jax.vmap(shuffled)(device_ids).astype(jnp.int32)
    entry = jnp.arange(R_MAX, dtype=jnp.int32)[None, :]
    filled = entry < counts[:, None]
    react = jnp.where(filled, chosen, -1).astype(jnp.int32)
    return react.reshape(-1)


def migration_lists(key):
    base = jax.random.fold_in(key, 13)
    device_ids = jnp.arange(N_DEV, dtype=jnp.int32)
    dropped = jax.random.randint(jax.random.fold_in(base, 1), (N_DEV, 2), 0, MCAP // 2 + 1)
    pick_lower = jax.random.randint(jax.random.fold_in(base, 2), (), 1, N_DEV)
    pick_upper = jax.random.randint(jax.random.fold_in(base, 3), (), 0, N_DEV - 1)
    downward = jnp.where(device_ids == pick_lower, MCAP, MCAP - dropped[:, 0])
    downward = jnp.where(device_ids == 0, 0, downward)
    upward = jnp.where(device_ids == pick_upper, MCAP, MCAP - dropped[:, 1])
    upward = jnp.where(device_ids == N_DEV - 1, 0, upward)

    def one_device(device, down_count, up_count):
        dkey = jax.random.fold_in(jax.random.fold_in(base, 4), device)
        shuffled = jax.random.permutation(jax.random.fold_in(dkey, 1), P_DEV).astype(jnp.int32)
        place = jnp.arange(P_DEV, dtype=jnp.int32)
        values = jnp.where(place < down_count, place, jnp.where(place < down_count + up_count, MCAP + place - down_count, -1))
        stay_rank = place - down_count - up_count
        random_cells = jax.random.randint(jax.random.fold_in(dkey, 2), (P_DEV,), 0, C_DEV)
        cells = jnp.where((stay_rank >= 0) & (stay_rank < C_DEV), stay_rank, random_cells)
        slot_out = jnp.zeros((P_DEV,), jnp.int32).at[shuffled].set(values.astype(jnp.int32))
        cell_out = jnp.zeros((P_DEV,), jnp.int32).at[shuffled].set(cells.astype(jnp.int32))
        return (slot_out, cell_out)
    slot_all, cell_all = jax.vmap(one_device)(device_ids, downward, upward)
    return (slot_all.reshape(-1), cell_all.reshape(-1))


def draw_react_list(key, part):
    return chemistry_lists(key)


def draw_move_slot(key, part):
    return migration_lists(key)[0]


def draw_cell_index(key, part):
    return migration_lists(key)[1]


def draw_jacobian_inverse(key, part):
    noise = jax.random.truncated_normal(key, -4.0, 4.0, (NB, S, S), jnp.float32)
    identity = jnp.eye(S, dtype=jnp.float32)[None, :, :]
    return (identity + 0.3 / math.sqrt(S) * noise).astype(jnp.bfloat16)


def place_ends(drawn, key, low, largest):
    longest = drawn.shape.index(max(drawn.shape))
    spots = []
    for shift in (0, 1):
        where = [jax.random.randint(jax.random.fold_in(key, axis), (), 0, length) for axis, length in enumerate(drawn.shape)]
        where[longest] = (where[longest] + shift) % drawn.shape[longest]
        spots.append(tuple(where))
    return drawn.at[spots[0]].set(low).at[spots[1]].set(largest)


def block_levels(rng, extent, shards, smallest, top_value):
    level, own = 1.0, jax.random.fold_in(rng, 6)
    for position, shards_of in shards:
        heights = jnp.exp(jax.random.uniform(jax.random.fold_in(own, position), (shards_of,), jnp.float32, smallest / len(shards), top_value / len(shards)))
        level = level * jnp.repeat(heights, extent[position] // shards_of).reshape([-1 if axis == position else 1 for axis in range(len(extent))])
    return level


def centred(rng, shape, scale, most, split=(), kind=jnp.bfloat16):
    loudness = block_levels(rng, shape, split, -0.22, 0.18) if split else 1.0
    entries = jax.random.normal(rng, shape, jnp.float32) * scale * loudness
    return jnp.minimum(jnp.maximum(entries, -most), most).astype(kind)


def setup_inputs(seed: int = 0) -> dict:
    arg_keys = jax.random.split(jax.random.key(seed), 12)
    return {
        "states": centred(arg_keys[0], (S, PARTICLES), 1.0, 6.0, ((1, 32),), jnp.float32),
        "particle_mass": jnp.clip(jnp.exp(math.log(10.0) - 2.3025851 * jax.random.uniform(arg_keys[1], (PARTICLES,), jnp.float32) ** block_levels(arg_keys[1], (PARTICLES,), ((0, 32),), -0.2, 0.2)), 1.0, 10.0),
        "bin_index": place_ends(jax.random.randint(arg_keys[2], (PARTICLES,), 0, NB), jax.random.fold_in(arg_keys[2], 1), 0, NB - 1).astype(jnp.int32),
        "cell_index": draw_cell_index(jax.random.fold_in(arg_keys[11], 71), 0),
        "move_slot": draw_move_slot(jax.random.fold_in(arg_keys[11], 71), 0),
        "react_list": draw_react_list(jax.random.fold_in(arg_keys[11], 71), 0),
        "rate_weights": centred(arg_keys[6], (R, S), S ** -0.5, 0.4375),
        "stoichiometry": centred(arg_keys[7], (S, R), R ** -0.5, 0.1875),
        "rate_scale": jnp.clip(jnp.exp(jax.random.uniform(arg_keys[8], (R,), jnp.float32, math.log(0.2), math.log(2.0))), 0.2, 2.0),
        "jacobian_inverse": draw_jacobian_inverse(jax.random.fold_in(arg_keys[11], 71), 0),
        "mixing_rate": jnp.clip(jnp.exp(math.log(8.0) - 2.7725887 * jax.random.uniform(arg_keys[10], (CELLS,), jnp.float32) ** block_levels(arg_keys[10], (CELLS,), ((0, 32),), -0.2, 0.2)), 0.5, 8.0),
    }


CHEM_STEP = 0.5
MIX_RATE = 0.5
EXACTLY = lax.Precision.HIGHEST


def newton(start, bin_mask, rate_weights, stoichiometry, rate_scale, jacobian_inverse):
    iterate = start
    mask_half = bin_mask.astype(jnp.bfloat16)
    for sweep in range(NEWTON):
        exponent = jnp.dot(rate_weights, iterate.astype(jnp.bfloat16), preferred_element_type=jnp.float32)
        reaction_rates = (rate_scale[:, None] * jax.nn.softplus(exponent)).astype(jnp.bfloat16)
        source_terms = jnp.dot(stoichiometry, reaction_rates, preferred_element_type=jnp.float32)
        residual = (iterate - start - CHEM_STEP * source_terms).astype(jnp.bfloat16)
        update = jnp.zeros_like(iterate)
        for level in range(NB):
            update = update + jnp.dot(jacobian_inverse[level], residual * mask_half[level], preferred_element_type=jnp.float32)
        iterate = iterate - update
    return iterate


def bin_table(bins):
    return (bins[None, :] == jnp.arange(NB, dtype=jnp.int32)[:, None]).astype(jnp.float32)


def cell_table(cells):
    return (cells[:, None] == jnp.arange(C_DEV, dtype=jnp.float32)[None, :]).astype(jnp.float32)


def spread(table, onehot):
    return lax.dot_general(table, onehot, (((1,), (1,)), ((), ())), precision=EXACTLY)


def mix_device(local, weights, cells, rates_dev):
    onehot = cell_table(cells)
    weighted = jnp.dot(local * weights[None, :], onehot, precision=EXACTLY)
    total = jnp.dot(weights[None, :], onehot, precision=EXACTLY)
    means = weighted / total
    factor = 1.0 - jnp.exp(-MIX_RATE * rates_dev)
    table = jnp.concatenate([means, factor[None, :]], axis=0)
    pulled = spread(table, onehot)
    mixed = local + (pulled[:-1] - local) * pulled[-1:]
    return jnp.where(weights[None, :] > 0, mixed, 0.0), means


def outgoing(device_states, masses, cells, slots):
    meta = jnp.stack([masses, cells.astype(jnp.float32)])
    to_lower = jnp.where((slots >= 0) & (slots < MCAP), slots, MCAP)
    to_upper = jnp.where(slots >= MCAP, slots - MCAP, MCAP)
    lower = jnp.zeros((S, MCAP), jnp.float32).at[:, to_lower].set(device_states, mode="drop")
    lower_meta = jnp.zeros((2, MCAP), jnp.float32).at[:, to_lower].set(meta, mode="drop")
    upper = jnp.zeros((S, MCAP), jnp.float32).at[:, to_upper].set(device_states, mode="drop")
    upper_meta = jnp.zeros((2, MCAP), jnp.float32).at[:, to_upper].set(meta, mode="drop")
    return lower, lower_meta, upper, upper_meta


def reference(states, particle_mass, bin_index, cell_index, move_slot, react_list, rate_weights, stoichiometry, rate_scale, jacobian_inverse, mixing_rate):
    live = react_list >= 0
    picked = jnp.nonzero(live, size=N_DEV * HELP_DEV)[0].astype(jnp.int32)
    columns = ((picked // R_MAX) * P_DEV + react_list[picked]).astype(jnp.int32)
    blocks = columns.reshape(N_DEV, HELP_DEV)

    def solve_block(block):
        start = jnp.take(states, block, axis=1)
        return newton(start, bin_table(jnp.take(bin_index, block)), rate_weights, stoichiometry, rate_scale, jacobian_inverse)

    solved = lax.map(solve_block, blocks)
    solved = jnp.transpose(solved, (1, 0, 2)).reshape(S, N_DEV * HELP_DEV)
    reacted = states.at[:, columns].set(solved)
    lower, lower_meta, upper, upper_meta = jax.vmap(outgoing, in_axes=(1, 0, 0, 0))(
        reacted.reshape(S, N_DEV, P_DEV), particle_mass.reshape(N_DEV, P_DEV),
        cell_index.reshape(N_DEV, P_DEV), move_slot.reshape(N_DEV, P_DEV))
    from_below = jnp.concatenate([jnp.zeros_like(upper[:1]), upper[:-1]], axis=0)
    below_meta = jnp.concatenate([jnp.zeros_like(upper_meta[:1]), upper_meta[:-1]], axis=0)
    from_above = jnp.concatenate([lower[1:], jnp.zeros_like(lower[:1])], axis=0)
    above_meta = jnp.concatenate([lower_meta[1:], jnp.zeros_like(lower_meta[:1])], axis=0)

    def mix_one(device):
        offset = (device * P_DEV).astype(jnp.int32)
        own = lax.dynamic_slice_in_dim(reacted, offset, P_DEV, 1)
        slots = lax.dynamic_slice_in_dim(move_slot, offset, P_DEV, 0)
        masses = lax.dynamic_slice_in_dim(particle_mass, offset, P_DEV, 0)
        cells = lax.dynamic_slice_in_dim(cell_index, offset, P_DEV, 0)
        rates_dev = lax.dynamic_slice_in_dim(mixing_rate, (device * C_DEV).astype(jnp.int32), C_DEV, 0)
        local = jnp.concatenate([own, from_below[device], from_above[device]], axis=1)
        weights = jnp.concatenate([jnp.where(slots < 0, masses, 0.0), below_meta[device][0], above_meta[device][0]])
        places = jnp.concatenate([cells.astype(jnp.float32), below_meta[device][1], above_meta[device][1]])
        return mix_device(local, weights, places, rates_dev)

    mixed, means = lax.map(mix_one, jnp.arange(N_DEV, dtype=jnp.int32))
    mixed_states = jnp.transpose(mixed, (1, 0, 2)).reshape(S, N_DEV * NLOC)
    cell_means = jnp.transpose(means, (1, 0, 2)).reshape(S, N_DEV * C_DEV)
    return mixed_states, cell_means
```

```python
import functools
import math
import jax
import jax.numpy as jnp
from jax import lax
from jax.experimental import pallas as pl
from jax.experimental.pallas import tpu as pltpu
from jax.sharding import PartitionSpec as P

NEWTON = 3
CHEM_STEP = 0.5
MIX_RATE = 0.5
BLK = 256
WIN = 384
NCOL = 512
ROWS = 192
META = 2 * ROWS
STACK = META + 16
F32, BF16 = jnp.float32, jnp.bfloat16


def nt(a, b):
    return lax.dot_general(a, b, (((1,), (1,)), ((), ())), preferred_element_type=F32)


def nn(a, b):
    return jnp.dot(a, b, preferred_element_type=F32)


def iota(shape, dim):
    return lax.broadcasted_iota(jnp.int32, shape, dim)


def halves(x):
    hi = x.astype(BF16)
    return hi, (x - hi.astype(F32)).astype(BF16)


def hot(row, size):
    return (iota((size, row.shape[1]), 0) == row).astype(F32).astype(BF16)


def row_of(ref, b):
    return jnp.concatenate([ref[pl.ds(BLK // 128 * b + i, 1), :] for i in range(BLK // 128)], axis=1)


def react_kernel(
    states, mass, bins, cells, slots, rlist, rate_w, stoich, scale, jac,
    reacted, lower, upper,
    rank, base_v, base_s, stack, start, picked_bins, d_hi, d_lo, ghot, moved, sem,
):
    species, count = states.shape
    tiles = count // 128
    blocks = count // BLK
    slot_count = moved.shape[1]
    r = rlist[...]
    listed = nt(hot(r >> 7, tiles), hot(r & 127, 128))
    upper_tri = (iota((128, 128), 0) < iota((128, 128), 1)).astype(F32).astype(BF16)
    lower_tri = (iota((tiles, tiles), 1) < iota((tiles, tiles), 0)).astype(F32).astype(BF16)
    listed_half = listed.astype(BF16)
    inside = nn(listed_half, upper_tri)
    before = jnp.sum(nn(lower_tri, listed_half), axis=1, keepdims=True)
    total = jnp.sum(jnp.sum(listed, axis=1, keepdims=True), axis=0, keepdims=True)
    rank[...] = jnp.where(listed > 0, inside + before, -1.0).astype(jnp.int32)
    base_v[...] = jnp.where(iota((tiles, 128), 1) == 0, before, total).astype(jnp.int32)
    copy = pltpu.make_async_copy(base_v, base_s, sem)
    copy.start()
    start[...] = jnp.zeros_like(start)
    picked_bins[...] = jnp.zeros_like(picked_bins)
    d_hi[...] = jnp.zeros_like(d_hi)
    d_lo[...] = jnp.zeros_like(d_lo)
    stack[...] = jnp.zeros_like(stack)
    moved[...] = jnp.zeros_like(moved)
    copy.wait()

    def window(b):
        return pl.multiple_of((base_s[BLK // 128 * b, 0] // 128) * 128, 128)

    def gather(b):
        at = pl.ds(pl.multiple_of(b * BLK, BLK), BLK)
        low = window(b)
        onehot = hot(row_of(rank, b) - low, WIN)
        ghot[pl.ds(pl.multiple_of(b * WIN, WIN), WIN), :] = onehot
        hi, lo = halves(states[:, at])
        binrow = jnp.broadcast_to(row_of(bins, b).astype(F32), (16, BLK)).astype(BF16)
        stack[0:species, :] = hi
        stack[ROWS : ROWS + species, :] = lo
        stack[META:STACK, :] = binrow
        got = nt(stack[...], onehot)
        start[:, pl.ds(low, WIN)] += got[:species] + got[ROWS : ROWS + species]
        picked_bins[:, pl.ds(low, WIN)] += got[META : META + 8]

    def gather_loop(i, c):
        gather(i)
        return c

    lax.fori_loop(0, blocks, gather_loop, 0)

    reactions = rate_w.shape[0]
    chunks = [(lo, min(256, reactions - lo)) for lo in range(0, reactions, 256)]
    log2e = math.log2(math.e)

    def solve(k, c):
        at = pl.ds(pl.multiple_of(k * NCOL, NCOL), NCOL)
        x0 = start[:, at]
        level = picked_bins[0:1, at]
        d = None
        for sweep in range(NEWTON):
            x = (x0 if d is None else x0 + d).astype(BF16)
            source = None
            for lo, size in chunks:
                u = nn(rate_w[lo : lo + size, :], x) * log2e
                soft = jnp.maximum(u, 0.0) + jnp.log2(1.0 + jnp.exp2(-jnp.abs(u)))
                rate = (soft * scale[lo : lo + size, 0:1]).astype(BF16)
                part = nn(stoich[:, lo : lo + size], rate)
                source = part if source is None else source + part
            residual = (-CHEM_STEP * source) if d is None else (d - CHEM_STEP * source)
            residual = residual.astype(BF16)
            update = nn(jac[0], residual)
            for b in range(1, jac.shape[0]):
                update = jnp.where(level == b, nn(jac[b], residual), update)
            d = -update if d is None else d - update
        hi, lo = halves(d)
        d_hi[:, at] = hi
        d_lo[:, at] = lo
        return c

    lax.fori_loop(0, (base_s[0, 1] + NCOL - 1) // NCOL, solve, 0)

    def finish(b, c):
        at = pl.ds(pl.multiple_of(b * BLK, BLK), BLK)
        low = window(b)
        onehot = ghot[pl.ds(pl.multiple_of(b * WIN, WIN), WIN), :]
        cols = pl.ds(low, WIN)
        new = states[:, at] + (nn(d_hi[:, cols], onehot) + nn(d_lo[:, cols], onehot))
        reacted[:, at] = new
        hi, lo = halves(new)
        m = row_of(mass, b)
        m_hi, m_lo = halves(m)
        which = iota((16, BLK), 0)
        meta = jnp.where(which == 0, m_hi.astype(F32), jnp.where(which == 1, m_lo.astype(F32), row_of(cells, b).astype(F32)))
        stack[0:species, :] = hi
        stack[ROWS : ROWS + species, :] = lo
        stack[META:STACK, :] = meta.astype(BF16)
        moved[...] += nt(stack[...], hot(row_of(slots, b), slot_count))
        return c

    lax.fori_loop(0, blocks, finish, 0)
    half = slot_count // 2
    for out, lo in ((lower, 0), (upper, half)):
        out[0:species, :] = moved[0:species, lo : lo + half] + moved[ROWS : ROWS + species, lo : lo + half]
        out[ROWS : ROWS + 8, :] = moved[META : META + 8, lo : lo + half]


def weighted_stack(stack, x, w, cell, n_cells):
    species = x.shape[0]
    hi, lo = halves(x * w)
    w_hi, w_lo = halves(w)
    which = iota((16, w.shape[1]), 0)
    stack[0:species, :] = hi
    stack[ROWS : ROWS + species, :] = lo
    stack[META:STACK, :] = jnp.where(which == 0, w_hi.astype(F32), w_lo.astype(F32)).astype(BF16)
    return nt(stack[...], hot(cell, n_cells))


def sums_kernel(reacted, mass, cells, slots, sums, stack):
    @pl.when(pl.program_id(0) == 0)
    def _():
        sums[...] = jnp.zeros_like(sums)
        stack[...] = jnp.zeros_like(stack)

    w = jnp.where(slots[...] < 0, mass[...], 0.0)
    sums[...] += weighted_stack(stack, reacted[...], w, cells[...], sums.shape[1])


def arrival(ref, species):
    meta = ref[ROWS : ROWS + 8, :]
    return ref[0:species, :], meta[0:1] + meta[1:2], meta[2:3].astype(jnp.int32)


def mix_kernel(reacted, mass, cells, slots, below, above, sums, mixing, mixed, means, stack, tab_hi, tab_lo):
    species = reacted.shape[0]
    n_cells = sums.shape[1]
    step = pl.program_id(0)
    last = pl.num_programs(0) - 1

    @pl.when(step == 0)
    def _():
        stack[...] = jnp.zeros_like(stack)
        acc = sums[...]
        for ref in (below, above):
            acc = acc + weighted_stack(stack, *arrival(ref, species), n_cells)
        mean = (acc[:species] + acc[ROWS : ROWS + species]) / (acc[META : META + 1] + acc[META + 1 : META + 2])
        means[...] = mean
        hi, lo = halves(mean)
        f_hi, f_lo = halves(jnp.broadcast_to(1.0 - jnp.exp(-MIX_RATE * mixing[...]), (16, n_cells)))
        tab_hi[0:ROWS, :] = jnp.zeros((ROWS, n_cells), BF16)
        tab_lo[0:ROWS, :] = jnp.zeros((ROWS, n_cells), BF16)
        tab_hi[0:species, :] = hi
        tab_lo[0:species, :] = lo
        tab_hi[ROWS:, :] = f_hi
        tab_lo[ROWS:, :] = f_lo

    def blend(x, w, cell):
        onehot = hot(cell, n_cells)
        pulled = nn(tab_hi[...], onehot) + nn(tab_lo[...], onehot)
        out = x + (pulled[:species] - x) * pulled[ROWS : ROWS + 1]
        return jnp.where(w > 0, out, 0.0)

    @pl.when(step < last)
    def _():
        mixed[...] = blend(reacted[...], jnp.where(slots[...] < 0, mass[...], 0.0), cells[...])

    @pl.when(step == last)
    def _():
        half = below.shape[1]
        mixed[:, 0:half] = blend(*arrival(below, species))
        mixed[:, half:] = blend(*arrival(above, species))


def body(
    states, particle_mass, bin_index, cell_index, move_slot, react_list,
    rate_weights, stoichiometry, rate_scale, jacobian_inverse, mixing_rate, slot_count,
):
    species, count = states.shape
    n_cells = mixing_rate.shape[0]
    listed = react_list.shape[0]
    tiles = count // 128
    wide = listed + max(WIN, NCOL)
    half = slot_count // 2
    square = lambda a: a.reshape(tiles, 128)
    line = lambda a: a.reshape(1, -1)
    scale = jnp.broadcast_to((rate_scale * math.log(2.0))[:, None], (rate_scale.shape[0], 128))
    reacted, lower, upper = pl.pallas_call(
        react_kernel,
        out_shape=(
            jax.ShapeDtypeStruct((species, count), F32),
            jax.ShapeDtypeStruct((ROWS + 8, half), F32),
            jax.ShapeDtypeStruct((ROWS + 8, half), F32),
        ),
        scratch_shapes=[
            pltpu.VMEM((tiles, 128), jnp.int32),
            pltpu.VMEM((tiles, 128), jnp.int32),
            pltpu.SMEM((tiles, 128), jnp.int32),
            pltpu.VMEM((STACK, BLK), BF16),
            pltpu.VMEM((species, wide), F32),
            pltpu.VMEM((8, wide), F32),
            pltpu.VMEM((species, wide), BF16),
            pltpu.VMEM((species, wide), BF16),
            pltpu.VMEM((count // BLK * WIN, BLK), BF16),
            pltpu.VMEM((STACK, slot_count), F32),
            pltpu.SemaphoreType.DMA,
        ],
        compiler_params=pltpu.CompilerParams(vmem_limit_bytes=56 * 2**20),
        name="react",
    )(
        states, square(particle_mass), square(bin_index), square(cell_index), square(move_slot),
        line(react_list), rate_weights, stoichiometry, scale, jacobian_inverse,
    )
    ranks = lax.axis_size("dev")
    below = lax.ppermute(upper, "dev", [(i, i + 1) for i in range(ranks - 1)])
    above = lax.ppermute(lower, "dev", [(i + 1, i) for i in range(ranks - 1)])
    width = slot_count
    steps = count // width
    own = lambda rows: pl.BlockSpec((rows, width), lambda i: (0, jnp.minimum(i, steps - 1)))
    whole = lambda shape: pl.BlockSpec(shape, lambda i: (0, 0))
    masses, cell_line, slot_line = line(particle_mass), line(cell_index), line(move_slot)
    sums = pl.pallas_call(
        sums_kernel,
        grid=(steps,),
        in_specs=[own(species), own(1), own(1), own(1)],
        out_specs=whole((STACK, n_cells)),
        out_shape=jax.ShapeDtypeStruct((STACK, n_cells), F32),
        scratch_shapes=[pltpu.VMEM((STACK, width), BF16)],
        compiler_params=pltpu.CompilerParams(vmem_limit_bytes=32 * 2**20),
        cost_estimate=pl.CostEstimate(flops=2 * STACK * count * n_cells, bytes_accessed=4 * species * count, transcendentals=0),
        name="sums",
    )(reacted, masses, cell_line, slot_line)
    mixed, means = pl.pallas_call(
        mix_kernel,
        grid=(steps + 1,),
        in_specs=[
            own(species), own(1), own(1), own(1),
            whole((ROWS + 8, half)), whole((ROWS + 8, half)), whole((STACK, n_cells)), whole((1, n_cells)),
        ],
        out_specs=(pl.BlockSpec((species, width), lambda i: (0, i)), whole((species, n_cells))),
        out_shape=(
            jax.ShapeDtypeStruct((species, count + slot_count), F32),
            jax.ShapeDtypeStruct((species, n_cells), F32),
        ),
        scratch_shapes=[
            pltpu.VMEM((STACK, half), BF16),
            pltpu.VMEM((ROWS + 16, n_cells), BF16),
            pltpu.VMEM((ROWS + 16, n_cells), BF16),
        ],
        compiler_params=pltpu.CompilerParams(vmem_limit_bytes=32 * 2**20),
        name="mix",
    )(reacted, masses, cell_line, slot_line, below, above, sums, line(mixing_rate))
    return mixed, means


MCAP = 512


def solution(mesh):
    each, all_of = P("dev"), P()
    return jax.shard_map(
        functools.partial(body, slot_count=2 * MCAP),
        mesh=mesh,
        in_specs=(P(None, "dev"), each, each, each, each, each, all_of, all_of, all_of, all_of, each),
        out_specs=(P(None, "dev"), P(None, "dev")),
        check_vma=False,
    )
```

```python
import functools
import math
import jax
import jax.numpy as jnp
from jax import lax
from jax.experimental import pallas as pl
from jax.experimental.pallas import tpu as pltpu
from jax.sharding import PartitionSpec as P

NEWTON = 3
CHEM_STEP = 0.5
MIX_RATE = 0.5
BLK = 256
WIN = 384
NCOL = 1024
ROWS = 192
META = ROWS
LOW = META + 16
STACK = LOW + ROWS
F32, BF16 = jnp.float32, jnp.bfloat16


def nt(a, b):
    return lax.dot_general(a, b, (((1,), (1,)), ((), ())), preferred_element_type=F32)


def nn(a, b):
    return jnp.dot(a, b, preferred_element_type=F32)


def iota(shape, dim):
    return lax.broadcasted_iota(jnp.int32, shape, dim)


def halves(x):
    hi = x.astype(BF16)
    return hi, (x - hi.astype(F32)).astype(BF16)


def hot(row, size):
    return (iota((size, row.shape[1]), 0) == row).astype(F32).astype(BF16)


def row_of(ref, b):
    return jnp.concatenate([ref[pl.ds(BLK // 128 * b + i, 1), :] for i in range(BLK // 128)], axis=1)


def window(first):
    return pl.multiple_of((first // 128) * 128, 128)


def ranks(mask):
    tiles = mask.shape[0]
    upper_tri = (iota((128, 128), 0) < iota((128, 128), 1)).astype(F32).astype(BF16)
    lower_tri = (iota((tiles, tiles), 1) < iota((tiles, tiles), 0)).astype(F32).astype(BF16)
    half = mask.astype(BF16)
    before = jnp.sum(nn(lower_tri, half), axis=1, keepdims=True)
    return jnp.where(mask > 0, nn(half, upper_tri) + before, -1.0).astype(jnp.int32), before


def rows16(rows, width):
    out = jnp.zeros((16, width), F32)
    which = iota((16, width), 0)
    for i, row in enumerate(rows):
        out = jnp.where(which == i, row.astype(F32), out)
    return out.astype(BF16)


def react_kernel(
    states, mass, bins, cells, slots, rlist, rate_wt, stoich, scale_row, jac3,
    lower, upper, rank, base_v, d_stack,
    move_rank, base_s, jac, rate_w, scale, stack, start, picked_bins, packed, sem,
):
    species, count = states.shape
    tiles = count // 128
    blocks = count // BLK
    slot_count = 2 * lower.shape[1]
    r = rlist[...]
    listed = nt(hot(r >> 7, tiles), hot(r & 127, 128))
    total = jnp.sum(jnp.sum(listed, axis=1, keepdims=True), axis=0, keepdims=True)
    rank[...], before = ranks(listed)
    move_rank[...], before_move = ranks((slots[...] >= 0).astype(F32))
    lane = iota((tiles, 128), 1)
    base_v[...] = jnp.where(lane == 0, before, jnp.where(lane == 1, total, before_move)).astype(jnp.int32)
    copy = pltpu.make_async_copy(base_v, base_s, sem)
    copy.start()
    start[...] = jnp.zeros_like(start)
    picked_bins[...] = jnp.zeros_like(picked_bins)
    d_stack[...] = jnp.zeros_like(d_stack)
    stack[...] = jnp.zeros_like(stack)
    packed[...] = jnp.zeros_like(packed)
    scale[...] = jnp.transpose(jnp.broadcast_to(scale_row[...] * math.log(2.0), (128, scale_row.shape[1])))
    rate_w[...] = jnp.transpose(rate_wt[...].astype(F32)).astype(BF16)
    for b in range(jac.shape[0]):
        jac[b] = jac3[:, b, :]
    copy.wait()

    def gather(b, c):
        at = pl.ds(pl.multiple_of(b * BLK, BLK), BLK)
        low = window(base_s[BLK // 128 * b, 0])
        low_move = window(base_s[BLK // 128 * b, 2])
        ranked = row_of(rank, b)
        slot = row_of(slots, b)
        hi, lo = halves(states[:, at])
        m_hi, m_lo = halves(row_of(mass, b))
        stack[0:species, :] = hi
        stack[META:LOW, :] = rows16(
            (m_hi, m_lo, row_of(cells, b), slot >> 2, slot & 3, ranked >> 4, ranked & 15, row_of(bins, b)), BLK
        )
        stack[LOW : LOW + species, :] = lo
        got = nt(stack[...], hot(ranked - low, WIN))
        gone = nt(stack[...], hot(row_of(move_rank, b) - low_move, WIN))
        start[:, pl.ds(low, WIN)] += got[:species] + got[LOW : LOW + species]
        picked_bins[:, pl.ds(low, WIN)] += got[META : META + 8]
        packed[:, pl.ds(low_move, WIN)] += gone
        return c

    lax.fori_loop(0, blocks, gather, 0)

    reactions = rate_w.shape[0]
    chunks = [(lo, min(256, reactions - lo)) for lo in range(0, reactions, 256)]
    log2e = math.log2(math.e)

    def solve(k, c):
        at = pl.ds(pl.multiple_of(k * NCOL, NCOL), NCOL)
        x0 = start[:, at]
        level = picked_bins[7:8, at]
        d = None
        for sweep in range(NEWTON):
            x = (x0 if d is None else x0 + d).astype(BF16)
            source = None
            for lo, size in chunks:
                u = nn(rate_w[lo : lo + size, :], x) * log2e
                soft = jnp.maximum(u, 0.0) + jnp.log2(1.0 + jnp.exp2(-jnp.abs(u)))
                rate = (soft * scale[lo : lo + size, 0:1]).astype(BF16)
                part = nn(stoich[:, lo : lo + size], rate)
                source = part if source is None else source + part
            residual = (-CHEM_STEP * source) if d is None else (d - CHEM_STEP * source)
            residual = residual.astype(BF16)
            update = nn(jac[0], residual)
            for b in range(1, jac.shape[0]):
                update = jnp.where(level == b, nn(jac[b], residual), update)
            d = -update if d is None else d - update
        hi, lo = halves(d)
        d_stack[0:species, at] = hi
        d_stack[ROWS : ROWS + species, at] = lo
        return c

    lax.fori_loop(0, (base_s[0, 1] + NCOL - 1) // NCOL, solve, 0)

    half = slot_count // 2
    most = rlist.shape[1]
    mine = packed[:, 0:slot_count]
    code = mine[META : META + 8]
    slot = jnp.where(code[0:1] > 0, 4.0 * code[3:4] + code[4:5], -1.0).astype(jnp.int32)
    mine = mine.astype(BF16)
    for out, first in ((lower, 0), (upper, half)):
        moved = nt(mine, hot(slot - first, half))
        code = moved[META : META + 8]
        source = jnp.where(code[0:1] > 0, 16.0 * code[5:6] + code[6:7], -1.0).astype(jnp.int32)
        delta = nn(d_stack[:, 0:most], hot(source, most))
        out[0:species, :] = moved[0:species] + moved[LOW : LOW + species] + (delta[0:species] + delta[ROWS : ROWS + species])
        out[ROWS : ROWS + 8, :] = code


def weighted_stack(stack, x, w, cell, n_cells):
    species = x.shape[0]
    hi, lo = halves(x * w)
    stack[0:species, :] = hi
    stack[META:LOW, :] = rows16(halves(w), w.shape[1])
    stack[LOW : LOW + species, :] = lo
    return nt(stack[...], hot(cell, n_cells))


def sums_kernel(base, states, rank, d_stack, mass, cells, slots, reacted, sums, stack):
    species, width = states.shape
    step = pl.program_id(0)

    @pl.when(step == 0)
    def _():
        sums[...] = jnp.zeros_like(sums)
        stack[...] = jnp.zeros_like(stack)

    for b in range(width // BLK):
        at = slice(b * BLK, (b + 1) * BLK)
        low = window(base[(step * (width // BLK) + b) * (BLK // 128), 0])
        delta = nn(d_stack[:, pl.ds(low, WIN)], hot(row_of(rank, b) - low, WIN))
        reacted[:, at] = states[:, at] + (delta[0:species] + delta[ROWS : ROWS + species])
    w = jnp.where(slots[...] < 0, mass[...], 0.0)
    sums[...] += weighted_stack(stack, reacted[...], w, cells[...], sums.shape[1])


def arrival(ref, species):
    meta = ref[ROWS : ROWS + 8, :]
    return ref[0:species, :], meta[0:1] + meta[1:2], meta[2:3].astype(jnp.int32)


def mix_kernel(reacted, mass, cells, slots, below, above, sums, mixing, mixed, means, stack, tab_hi, tab_lo):
    species = reacted.shape[0]
    n_cells = sums.shape[1]
    step = pl.program_id(0)
    last = pl.num_programs(0) - 1

    @pl.when(step == 0)
    def _():
        stack[...] = jnp.zeros_like(stack)
        acc = sums[...]
        for ref in (below, above):
            acc = acc + weighted_stack(stack, *arrival(ref, species), n_cells)
        mean = (acc[:species] + acc[LOW : LOW + species]) / (acc[META : META + 1] + acc[META + 1 : META + 2])
        means[...] = mean
        hi, lo = halves(mean)
        f_hi, f_lo = halves(jnp.broadcast_to(1.0 - jnp.exp(-MIX_RATE * mixing[...]), (16, n_cells)))
        tab_hi[0:ROWS, :] = jnp.zeros((ROWS, n_cells), BF16)
        tab_lo[0:ROWS, :] = jnp.zeros((ROWS, n_cells), BF16)
        tab_hi[0:species, :] = hi
        tab_lo[0:species, :] = lo
        tab_hi[ROWS:, :] = f_hi
        tab_lo[ROWS:, :] = f_lo

    def blend(x, w, cell):
        onehot = hot(cell, n_cells)
        pulled = nn(tab_hi[...], onehot) + nn(tab_lo[...], onehot)
        out = x + (pulled[:species] - x) * pulled[ROWS : ROWS + 1]
        return jnp.where(w > 0, out, 0.0)

    @pl.when(step < last)
    def _():
        mixed[...] = blend(reacted[...], jnp.where(slots[...] < 0, mass[...], 0.0), cells[...])

    @pl.when(step == last)
    def _():
        half = below.shape[1]
        mixed[:, 0:half] = blend(*arrival(below, species))
        mixed[:, half:] = blend(*arrival(above, species))


def body(
    states, particle_mass, bin_index, cell_index, move_slot, react_list,
    rate_weights, stoichiometry, rate_scale, jacobian_inverse, mixing_rate, slot_count,
):
    species, count = states.shape
    n_cells = mixing_rate.shape[0]
    listed = react_list.shape[0]
    tiles = count // 128
    wide = listed + WIN
    half = slot_count // 2
    square = lambda a: a.reshape(tiles, 128)
    line = lambda a: a.reshape(1, -1)
    scale = rate_scale.reshape(1, -1)
    lower, upper, rank, base, d_stack = pl.pallas_call(
        react_kernel,
        out_shape=(
            jax.ShapeDtypeStruct((ROWS + 8, half), F32),
            jax.ShapeDtypeStruct((ROWS + 8, half), F32),
            jax.ShapeDtypeStruct((tiles, 128), jnp.int32),
            jax.ShapeDtypeStruct((tiles, 128), jnp.int32),
            jax.ShapeDtypeStruct((2 * ROWS, wide), BF16),
        ),
        scratch_shapes=[
            pltpu.VMEM((tiles, 128), jnp.int32),
            pltpu.SMEM((tiles, 128), jnp.int32),
            pltpu.VMEM(jacobian_inverse.shape, BF16),
            pltpu.VMEM(rate_weights.shape, BF16),
            pltpu.VMEM((rate_scale.shape[0], 128), F32),
            pltpu.VMEM((STACK, BLK), BF16),
            pltpu.VMEM((species, wide), F32),
            pltpu.VMEM((8, wide), F32),
            pltpu.VMEM((STACK, slot_count + WIN), F32),
            pltpu.SemaphoreType.DMA,
        ],
        compiler_params=pltpu.CompilerParams(vmem_limit_bytes=56 * 2**20),
        name="react",
    )(
        states, square(particle_mass), square(bin_index), square(cell_index), square(move_slot),
        line(react_list), rate_weights.T, stoichiometry, scale, jnp.transpose(jacobian_inverse, (1, 0, 2)),
    )
    devices = lax.axis_size("dev")
    below = lax.ppermute(upper, "dev", [(i, i + 1) for i in range(devices - 1)])
    above = lax.ppermute(lower, "dev", [(i + 1, i) for i in range(devices - 1)])
    width = slot_count
    steps = count // width
    own = lambda rows: pl.BlockSpec((rows, width), lambda i: (0, jnp.minimum(i, steps - 1)))
    whole = lambda shape: pl.BlockSpec(shape, lambda i: (0, 0))
    masses, cell_line, slot_line = line(particle_mass), line(cell_index), line(move_slot)
    reacted, sums = pl.pallas_call(
        sums_kernel,
        grid=(steps,),
        in_specs=[
            pl.BlockSpec(memory_space=pltpu.SMEM), own(species), pl.BlockSpec((width // 128, 128), lambda i: (i, 0)),
            whole((2 * ROWS, wide)), own(1), own(1), own(1),
        ],
        out_specs=(own(species), whole((STACK, n_cells))),
        out_shape=(jax.ShapeDtypeStruct((species, count), F32), jax.ShapeDtypeStruct((STACK, n_cells), F32)),
        scratch_shapes=[pltpu.VMEM((STACK, width), BF16)],
        compiler_params=pltpu.CompilerParams(vmem_limit_bytes=40 * 2**20),
        cost_estimate=pl.CostEstimate(
            flops=2 * STACK * count * (n_cells + WIN), bytes_accessed=8 * species * count, transcendentals=0
        ),
        name="sums",
    )(base, states, rank, d_stack, masses, cell_line, slot_line)
    mixed, means = pl.pallas_call(
        mix_kernel,
        grid=(steps + 1,),
        in_specs=[
            own(species), own(1), own(1), own(1),
            whole((ROWS + 8, half)), whole((ROWS + 8, half)), whole((STACK, n_cells)), whole((1, n_cells)),
        ],
        out_specs=(pl.BlockSpec((species, width), lambda i: (0, i)), whole((species, n_cells))),
        out_shape=(
            jax.ShapeDtypeStruct((species, count + slot_count), F32),
            jax.ShapeDtypeStruct((species, n_cells), F32),
        ),
        scratch_shapes=[
            pltpu.VMEM((STACK, half), BF16),
            pltpu.VMEM((ROWS + 16, n_cells), BF16),
            pltpu.VMEM((ROWS + 16, n_cells), BF16),
        ],
        compiler_params=pltpu.CompilerParams(vmem_limit_bytes=32 * 2**20),
        name="mix",
    )(reacted, masses, cell_line, slot_line, below, above, sums, line(mixing_rate))
    return mixed, means


MCAP = 512


def solution(mesh):
    each, all_of = P("dev"), P()
    return jax.shard_map(
        functools.partial(body, slot_count=2 * MCAP),
        mesh=mesh,
        in_specs=(P(None, "dev"), each, each, each, each, each, all_of, all_of, all_of, all_of, each),
        out_specs=(P(None, "dev"), P(None, "dev")),
        check_vma=False,
    )
```
